256 devices in a mesh: tok: 32 (over x, z), head: 8 (over y, core).
Axes of the slice: x: 4, y: 4, z: 8, core: 2. Of those that a mesh axis runs over, the one named last changes fastest.
Arguments:
- query: bfloat16 [32768, 5120], P(('tok', 'head')), may hold values from -40 to 40
- key: bfloat16 [32768, 5120], P(('tok', 'head')), may hold values from -5 to 5
- value: bfloat16 [32768, 5120], P(('tok', 'head')), may hold values from -6 to 6
- out_grad: bfloat16 [32768, 5120], P(('tok', 'head')), may hold values from -6 to 6
- intersection: int32 [32, 16], replicated, may hold values from -1 to 1023, as said below
- counts: int32 [32], replicated, may hold values from 12 to 16, as said below
Outputs:
- query_grad: bfloat16 [32768, 5120], P(('tok', 'head'))
- key_grad: bfloat16 [32768, 5120], P(('tok', 'head'))
- value_grad: bfloat16 [32768, 5120], P(('tok', 'head'))
The draws below stay inside these ranges and needn't reach their ends.
Inputs may be any that keep to these rules, and one draw needn't show every extreme that they name: `intersection`: entries j < counts[f] of row f name blocks of distinct frames, none of them f itself; the others are -1. `counts`: some frame retrieves 16 blocks.
All inputs are finite; a program needn't handle non-finite values.
Results may differ from the reference program's by a relative error of at most 0.027.
Values may be sent and summed in bfloat16 or wider, within the bound.
No kernel may reach another device: no remote copies, remote signals or barrier semaphores. Data moves between devices by JAX's collectives and lax.ppermute only.
A program may use at most 64 MiB of HBM per device.

```python
import math
import jax
import jax.numpy as jnp
from jax import lax

D = 5120
HEADS = 40
HD = 128
TOK_DEV = 128
FBLK = 32
FRAMES = 32
BLK_DEV = 32
MEMD = 16
TOKENS = 32768
N_TOK = 32
N_HEAD = 8


def frame_lists(key):
    key = jax.random.fold_in(key, 101)
    row_keys = jax.random.split(key, FRAMES)
    offsets = jax.vmap(lambda one: jax.random.permutation(one, FRAMES - 1))(row_keys)[:, :MEMD]
    frames = jnp.arange(FRAMES, dtype=jnp.int32)
    source = (frames[:, None] + 1 + offsets.astype(jnp.int32)) % FRAMES
    blocks = jax.random.randint(jax.random.fold_in(key, 103), (FRAMES, MEMD), 0, BLK_DEV)
    number = jax.random.randint(jax.random.fold_in(key, 107), (FRAMES,), MEMD - MEMD // 4, MEMD + 1)
    fullest = jax.random.randint(jax.random.fold_in(key, 109), (), 0, FRAMES)
    number = jnp.where(frames == fullest, MEMD, number).astype(jnp.int32)
    slots = jnp.arange(MEMD, dtype=jnp.int32)
    ids = jnp.where(slots[None, :] < number[:, None], source * BLK_DEV + blocks, -1)
    return (ids.astype(jnp.int32), number)


def draw_intersection(key, part):
    ids, number = frame_lists(key)
    return ids


def draw_counts(key, part):
    ids, number = frame_lists(key)
    return number


def draw_key(key, part):
    key = jax.random.fold_in(key, 21)
    base = jnp.clip(jax.random.normal(key, (TOKENS, D), jnp.float32), -5.0, 5.0)
    return base.astype(jnp.bfloat16)


def draw_query(key, part):
    key = jax.random.fold_in(key, 11)
    own = jnp.clip(2.5 * jax.random.normal(key, (TOKENS, D), jnp.float32), -15.0, 15.0)
    return own.astype(jnp.bfloat16)


def levels(key, extent, shards, smallest, top_value):
    factor_of, own = 1.0, jax.random.fold_in(key, 6)
    for axis_at, parts in shards:
        steps = jnp.exp(jax.random.uniform(jax.random.fold_in(own, axis_at), (parts,), jnp.float32, smallest / len(shards), top_value / len(shards)))
        factor_of = factor_of * jnp.repeat(steps, extent[axis_at] // parts).reshape([-1 if axis == axis_at else 1 for axis in range(len(extent))])
    return factor_of


def scatter_about(own_key, extent, width, bound, cuts=(), kind=jnp.bfloat16):
    values = jax.random.normal(own_key, extent, jnp.float32) * width
    if len(cuts) > 0:
        values = levels(own_key, extent, cuts, -0.22, 0.18) * values
    return jnp.clip(values, min=-bound, max=bound).astype(kind)


def setup_inputs(seed: int = 0) -> dict:
    streams_of = jax.random.split(jax.random.key(seed), 7)
    query = draw_query(jax.random.fold_in(streams_of[6], 71), 0)
    key = draw_key(jax.random.fold_in(streams_of[6], 71), 0)
    value = scatter_about(streams_of[2], (TOKENS, D), 1.0, 6.0, ((0, 256),))
    out_grad = scatter_about(streams_of[3], (TOKENS, D), 1.0, 6.0, ((0, 256),))
    intersection = draw_intersection(jax.random.fold_in(streams_of[6], 71), 0)
    counts = draw_counts(jax.random.fold_in(streams_of[6], 71), 0)
    return {"query": query, "key": key, "value": value, "out_grad": out_grad, "intersection": intersection, "counts": counts}


def score_rows(qh, kh, keymask):
    scale = 1.0 / math.sqrt(HD)
    scores = jnp.dot(qh, kh.T, preferred_element_type=jnp.float32) * scale
    return jnp.where(keymask[None, :], scores, -jnp.inf)

def head_forward(qh, kh, vh, keymask):
    scores = score_rows(qh, kh, keymask)
    top = lax.optimization_barrier(jnp.max(scores, axis=1, keepdims=True))
    expo = jnp.exp(scores - top)
    total = lax.optimization_barrier(jnp.sum(expo, axis=1, keepdims=True))
    weights = (expo / total).astype(jnp.bfloat16)
    output = jnp.dot(weights, vh, preferred_element_type=jnp.float32).astype(jnp.bfloat16)
    return (output, top + jnp.log(total))

def head_backward(qh, kh, vh, dh, keymask, output, logsum):
    scale = 1.0 / math.sqrt(HD)
    scores = score_rows(qh, kh, keymask)
    prob = jnp.exp(scores - logsum)
    weights = prob.astype(jnp.bfloat16)
    dprob = jnp.dot(dh, vh.T, preferred_element_type=jnp.float32)
    delta = lax.optimization_barrier(jnp.sum(dh.astype(jnp.float32) * output.astype(jnp.float32), axis=1, keepdims=True))
    dscore = (prob * (dprob - delta)).astype(jnp.bfloat16)
    dquery = (jnp.dot(dscore, kh, preferred_element_type=jnp.float32) * scale).astype(jnp.bfloat16)
    dkey = jnp.dot(dscore.T, qh, preferred_element_type=jnp.float32) * scale
    dvalue = jnp.dot(weights.T, dh, preferred_element_type=jnp.float32)
    return (dquery, dkey, dvalue)

def reference(query, key, value, out_grad, intersection, counts):
    frame_tok = TOK_DEV * N_HEAD
    nblk = frame_tok // FBLK
    kblocks = key.reshape(N_TOK * nblk, FBLK, D)
    vblocks = value.reshape(N_TOK * nblk, FBLK, D)

    def frame_fn(frame):

        def rows(x):
            return lax.dynamic_slice_in_dim(x, frame * frame_tok, frame_tok, 0)
        qf, kf, vf, df = (rows(query), rows(key), rows(value), rows(out_grad))
        ids = lax.dynamic_index_in_dim(intersection, frame, 0, keepdims=False)
        limit = lax.dynamic_index_in_dim(counts, frame, 0, keepdims=False)
        live = jnp.arange(MEMD, dtype=jnp.int32) < limit
        safe = jnp.maximum(ids, 0).astype(jnp.int32)
        keys = jnp.concatenate([kf, kblocks[safe].reshape(MEMD * FBLK, D)], axis=0)
        vals = jnp.concatenate([vf, vblocks[safe].reshape(MEMD * FBLK, D)], axis=0)
        keymask = jnp.concatenate([jnp.ones((frame_tok,), bool), jnp.repeat(live, FBLK)])

        def head_fn(head):

            def cols(x):
                return lax.dynamic_slice_in_dim(x, head * HD, HD, 1)
            qh, kh, vh, dh = (cols(qf), cols(keys), cols(vals), cols(df))
            output, logsum = head_forward(qh, kh, vh, keymask)
            return head_backward(qh, kh, vh, dh, keymask, output, logsum)
        dquery, dkey, dvalue = lax.map(head_fn, jnp.arange(HEADS, dtype=jnp.int32))

        def joined(x):
            return jnp.transpose(x, (1, 0, 2)).reshape(x.shape[1], D)
        dquery, dkey, dvalue = (joined(dquery), joined(dkey), joined(dvalue))
        mem_k = dkey[frame_tok:].astype(jnp.bfloat16).reshape(MEMD, FBLK, D)
        mem_v = dvalue[frame_tok:].astype(jnp.bfloat16).reshape(MEMD, FBLK, D)
        return (dquery, dkey[:frame_tok], dvalue[:frame_tok], mem_k, mem_v, safe, live)
    dq, dkl, dvl, mem_k, mem_v, safe, live = lax.map(frame_fn, jnp.arange(N_TOK, dtype=jnp.int32))
    flat_ids = safe.reshape(-1)
    weight = live.reshape(-1).astype(jnp.float32)[:, None, None]
    total_k = dkl.reshape(N_TOK * nblk, FBLK, D).at[flat_ids].add(mem_k.reshape(-1, FBLK, D).astype(jnp.float32) * weight)
    total_v = dvl.reshape(N_TOK * nblk, FBLK, D).at[flat_ids].add(mem_v.reshape(-1, FBLK, D).astype(jnp.float32) * weight)
    return (dq.reshape(TOKENS, D), total_k.reshape(TOKENS, D).astype(jnp.bfloat16), total_v.reshape(TOKENS, D).astype(jnp.bfloat16))
```

```python
import functools
import math

import jax
import jax.numpy as jnp
from jax import lax
from jax.experimental import pallas as pl
from jax.experimental.pallas import tpu as pltpu
from jax.sharding import PartitionSpec as P

HD = 128
FBLK = 32
SCALE = 1.0 / math.sqrt(HD)
LOG2E = math.log2(math.e)
VMEM_LIMIT = 48 * 2**20
NN = (((1,), (0,)), ((), ()))
NT = (((1,), (1,)), ((), ()))
TN = (((0,), (0,)), ((), ()))
F32 = jnp.float32
BF16 = jnp.bfloat16


def in_vmem():
    return pl.BlockSpec(memory_space=pltpu.VMEM)


def in_smem():
    return pl.BlockSpec(memory_space=pltpu.SMEM)


def dot(a, b, dims):
    return lax.dot_general(a, b, dims, preferred_element_type=F32)


def attend_kernel(pieces, memd, tq, kc, lists_ref, kv_ref, *refs):
    qd_refs, recv_ref = refs[:pieces], refs[pieces]
    dq_ref, own_ref, ret_ref = refs[pieces + 1 : pieces + 4]
    k_s, v_s, q_s, d_s, s_s, e_s, gk_s, gv_s = refs[pieces + 4 :]
    tok = kv_ref.shape[2]
    own = tok * pieces
    total = own + memd * FBLK
    count = lists_ref[memd]

    def head(h, _):
        hs = pl.ds(pl.multiple_of(h * HD, HD), HD)
        for i in range(pieces):
            rows = slice(i * tok, (i + 1) * tok)
            k_s[rows] = kv_ref[i, 0, :, hs]
            v_s[rows] = kv_ref[i, 1, :, hs]
            q_s[rows] = qd_refs[i][0, :, hs]
            d_s[rows] = qd_refs[i][1, :, hs]
        for j in range(memd):
            rows = slice(own + j * FBLK, own + (j + 1) * FBLK)
            k_s[rows] = recv_ref[lists_ref[j], 0, :, hs]
            v_s[rows] = recv_ref[lists_ref[j], 1, :, hs]

        def tile(t, _):
            qs = pl.ds(pl.multiple_of(t * tq, tq), tq)
            q, d = q_s[qs, :], d_s[qs, :]
            top = jnp.full((1, tq), -jnp.inf, F32)
            for c in range(0, total, kc):
                s = dot(k_s[c : c + kc], q, NT)
                if c + kc > own:
                    entry = (lax.broadcasted_iota(jnp.int32, (kc, tq), 0) + (c - own)) // FBLK
                    s = jnp.where(entry < count, s, -jnp.inf)
                s_s[c : c + kc] = s
                top = jnp.maximum(top, jnp.max(s, axis=0, keepdims=True))
            norm = jnp.zeros((1, tq), F32)
            delta = jnp.zeros((1, tq), F32)
            for c in range(0, total, kc):
                e = jnp.exp2((s_s[c : c + kc] - top) * (SCALE * LOG2E))
                dp = dot(v_s[c : c + kc], d, NT)
                s_s[c : c + kc] = e
                e_s[c : c + kc] = dp
                norm = norm + jnp.sum(e, axis=0, keepdims=True)
                delta = delta + jnp.sum(e * dp, axis=0, keepdims=True)
            inv = 1.0 / norm
            delta = delta * inv
            dq = jnp.zeros((tq, HD), F32)
            for c in range(0, total, kc):
                p = s_s[c : c + kc] * inv
                ds = (p * (e_s[c : c + kc] - delta)).astype(BF16)
                gv = dot(p.astype(BF16), d, NN)
                gk = dot(ds, q, NN)
                gk_s[c : c + kc] = jnp.where(t == 0, gk, gk_s[c : c + kc] + gk)
                gv_s[c : c + kc] = jnp.where(t == 0, gv, gv_s[c : c + kc] + gv)
                dq = dq + dot(ds, k_s[c : c + kc], TN)
            dq_ref[qs, hs] = (dq * SCALE).astype(BF16)
            return 0

        lax.fori_loop(0, own // tq, tile, 0)
        own_ref[0, :, hs] = gk_s[:own] * SCALE
        own_ref[1, :, hs] = gv_s[:own]
        for j in range(memd):
            rows = slice(own + j * FBLK, own + (j + 1) * FBLK)

            @pl.when(j < count)
            def _():
                ret_ref[lists_ref[j], 0, :, hs] = (gk_s[rows] * SCALE).astype(BF16)
                ret_ref[lists_ref[j], 1, :, hs] = gv_s[rows].astype(BF16)

        return 0

    lax.fori_loop(0, kv_ref.shape[3] // HD, head, 0)


def attend(lists, kv, qd, recv, tq=512, kc=512):
    pieces, _, tok, width = kv.shape
    memd, slots = lists.shape[0] - 1, recv.shape[0]
    own = pieces * tok
    total = own + memd * FBLK
    return pl.pallas_call(
        functools.partial(attend_kernel, pieces, memd, tq, kc),
        out_shape=(
            jax.ShapeDtypeStruct((own, width), BF16),
            jax.ShapeDtypeStruct((2, own, width), F32),
            jax.ShapeDtypeStruct((slots, 2, FBLK, width), BF16),
        ),
        in_specs=[in_smem()] + [in_vmem()] * (pieces + 2),
        out_specs=(in_vmem(),) * 3,
        scratch_shapes=[
            pltpu.VMEM((total, HD), BF16),
            pltpu.VMEM((total, HD), BF16),
            pltpu.VMEM((own, HD), BF16),
            pltpu.VMEM((own, HD), BF16),
            pltpu.VMEM((total, tq), F32),
            pltpu.VMEM((total, tq), F32),
            pltpu.VMEM((total, HD), F32),
            pltpu.VMEM((total, HD), F32),
        ],
        compiler_params=pltpu.CompilerParams(vmem_limit_bytes=VMEM_LIMIT),
        cost_estimate=pl.CostEstimate(
            flops=10 * own * total * width, bytes_accessed=16 * own * width, transcendentals=own * total * width // HD
        ),
        name="attend",
    )(lists, kv, *qd, recv)


def pick_kernel(picks_ref, kv_ref, out_ref):
    def slot(s, _):
        block = picks_ref[s]
        rows = pl.ds(pl.multiple_of(lax.rem(block, 4) * FBLK, FBLK), FBLK)
        out_ref[s] = kv_ref[lax.div(block, 4), :, rows, :]
        return 0

    lax.fori_loop(0, out_ref.shape[0], slot, 0)


def pick(picks, kv, slots):
    return pl.pallas_call(
        pick_kernel,
        out_shape=jax.ShapeDtypeStruct((slots, 2, FBLK, kv.shape[3]), BF16),
        in_specs=[in_smem(), in_vmem()],
        out_specs=in_vmem(),
        compiler_params=pltpu.CompilerParams(vmem_limit_bytes=VMEM_LIMIT),
        name="pick",
    )(picks, kv)


def collect_kernel(picks_ref, wanted_ref, own_ref, back_ref, out_ref, acc):
    acc[...] = own_ref[...]

    def slot(s, _):
        @pl.when(wanted_ref[s] != 0)
        def _():
            rows = pl.ds(pl.multiple_of(picks_ref[s] * FBLK, FBLK), FBLK)
            acc[:, rows, :] += back_ref[s].astype(F32)

        return 0

    lax.fori_loop(0, back_ref.shape[0], slot, 0)
    tok = out_ref.shape[2]
    for i in range(out_ref.shape[0]):
        out_ref[i] = acc[:, i * tok : (i + 1) * tok, :].astype(BF16)


def collect(picks, wanted, own, back, pieces):
    _, rows, width = own.shape
    return pl.pallas_call(
        collect_kernel,
        out_shape=jax.ShapeDtypeStruct((pieces, 2, rows // pieces, width), BF16),
        in_specs=[in_smem(), in_smem(), in_vmem(), in_vmem()],
        out_specs=in_vmem(),
        scratch_shapes=[pltpu.VMEM(own.shape, F32)],
        compiler_params=pltpu.CompilerParams(vmem_limit_bytes=VMEM_LIMIT),
        name="collect",
    )(picks, wanted, own, back)


def place_kernel(count, me_ref, *refs):
    for k, ref in enumerate(refs[:count]):
        width = ref.shape[-1]
        at = pl.multiple_of((me_ref[0] ^ k) * width, HD)
        for i, out_ref in enumerate(refs[count:]):
            out_ref[:, pl.ds(at, width)] = ref[i]


def place(me, pieces):
    arrays, tok, width = pieces[0].shape
    return pl.pallas_call(
        functools.partial(place_kernel, len(pieces)),
        out_shape=[jax.ShapeDtypeStruct((tok, width * len(pieces)), BF16)] * arrays,
        in_specs=[in_smem()] + [in_vmem()] * len(pieces),
        out_specs=[in_vmem()] * arrays,
        compiler_params=pltpu.CompilerParams(vmem_limit_bytes=VMEM_LIMIT),
        name="place",
    )(me, *pieces)


def swap(parts):
    got = {0: parts[0]}
    for k in (4, 5, 2, 3, 6, 7, 1):
        got[k] = lax.ppermute(parts[k], "head", [(i, i ^ k) for i in range(len(parts))])
    return [got[k] for k in range(len(parts))]


def body(query, key, value, out_grad, intersection, counts):
    frames, heads = lax.axis_size("tok"), lax.axis_size("head")
    frame, me = lax.axis_index("tok"), lax.axis_index("head")
    tok, width = query.shape
    cols = width // heads
    blk_tok = tok // FBLK
    blk_dev = blk_tok * heads
    memd = intersection.shape[1]

    def to_heads(a, b):
        return swap(
            [
                jnp.stack([lax.dynamic_slice(x, (0, (me ^ k) * cols), (tok, cols)) for x in (a, b)])
                for k in range(heads)
            ]
        )

    slots = jnp.arange(memd, dtype=jnp.int32)
    live = slots[None, :] < counts[:, None]
    safe = jnp.maximum(intersection, 0)
    mine = live & (safe // blk_dev == frame)
    wanted = jnp.any(mine, axis=1).astype(jnp.int32)
    block = jnp.sum(jnp.where(mine, safe % blk_dev, 0), axis=1)
    picks = ((block // blk_tok) ^ me) * blk_tok + block % blk_tok
    my_ids = lax.dynamic_index_in_dim(safe, frame, 0, keepdims=False) // blk_dev
    my_count = lax.dynamic_index_in_dim(counts, frame, 0, keepdims=True)
    lists = jnp.concatenate([my_ids, my_count])

    kv = jnp.stack(to_heads(key, value))
    sent = pick(picks, kv, frames)
    query, out_grad, sent = lax.optimization_barrier((query, out_grad, sent))
    recv = lax.all_to_all(sent, "tok", split_axis=0, concat_axis=0, tiled=True)
    qd = to_heads(query, out_grad)
    dq, own, ret = attend(lists, kv, qd, recv)
    back = lax.all_to_all(ret, "tok", split_axis=0, concat_axis=0, tiled=True)
    me1 = me[None]
    dq_out = place(me1, swap([dq[None, k * tok : (k + 1) * tok] for k in range(heads)]))
    dkv = collect(picks, wanted, own, back, heads)
    dkv = swap([dkv[k] for k in range(heads)])
    return (*dq_out, *place(me1, dkv))


def solution(mesh):
    rows = P(("tok", "head"), None)
    return jax.shard_map(
        body,
        mesh=mesh,
        in_specs=(rows, rows, rows, rows, P(), P()),
        out_specs=(rows, rows, rows),
        check_vma=False,
    )
```

```python
import functools
import math

import jax
import jax.numpy as jnp
from jax import lax
from jax.experimental import pallas as pl
from jax.experimental.pallas import tpu as pltpu
from jax.sharding import PartitionSpec as P

HD = 128
FBLK = 32
LEAST_LIVE = 12
SCALE = 1.0 / math.sqrt(HD)
TO_EXP2 = SCALE * math.log2(math.e)
VMEM_LIMIT = 40 * 2**20
MOST_VMEM = 60 * 2**20
SMALL_LIMIT = 16 * 2**20
NN = (((1,), (0,)), ((), ()))
NT = (((1,), (1,)), ((), ()))
TN = (((0,), (0,)), ((), ()))
F32 = jnp.float32
BF16 = jnp.bfloat16


def smem():
    return pl.BlockSpec(memory_space=pltpu.SMEM)


def anywhere():
    return pl.BlockSpec(memory_space=pl.ANY)


def per_head(shape):
    lead = len(shape) - 3
    return pl.BlockSpec((*shape[:lead], None, *shape[-2:]), lambda h: (0,) * lead + (h, 0, 0))


def vmem():
    return pl.BlockSpec(memory_space=pltpu.VMEM)


def stat_block(own):
    return pl.BlockSpec((1, 8, own), lambda h: (h, 0, 0))


def params():
    return pltpu.CompilerParams(vmem_limit_bytes=VMEM_LIMIT, dimension_semantics=("arbitrary",))


def dot(a, b, dims):
    return lax.dot_general(a, b, dims, preferred_element_type=F32)


def column_sum(x):
    return jnp.sum(x, axis=0, keepdims=True)


def rows_of(ref, which, lo, count):
    tok = ref.shape[2]
    return ref[which, lo // tok : (lo + count) // tok].reshape(count, HD)


def load_memory(lists_ref, recv_ref, k_s, v_s):
    for j in range(k_s.shape[0] // FBLK):
        k_s[j * FBLK : (j + 1) * FBLK] = recv_ref[lists_ref[j], 0]
        v_s[j * FBLK : (j + 1) * FBLK] = recv_ref[lists_ref[j], 1]


def masked(s, count, first=0):
    row = lax.broadcasted_iota(jnp.int32, s.shape, 0)
    return jnp.where(row < count * FBLK - first, s, -jnp.inf)


def own_stats_kernel(kc, kv_ref, qd_ref, stat_ref, s_s):
    own = s_s.shape[0]
    q, d = rows_of(qd_ref, 0, 0, own), rows_of(qd_ref, 1, 0, own)
    top = jnp.full((1, own), -jnp.inf, F32)
    for c in range(0, own, kc):
        s = dot(rows_of(kv_ref, 0, c, kc), q, NT)
        s_s[c : c + kc] = s
        top = jnp.maximum(top, jnp.max(s, axis=0, keepdims=True))
    norm = jnp.zeros((1, own), F32)
    mix = jnp.zeros((1, own), F32)
    for c in range(0, own, kc):
        e = jnp.exp2((s_s[c : c + kc] - top) * TO_EXP2)
        norm = norm + column_sum(e)
        mix = mix + column_sum(e * dot(rows_of(kv_ref, 1, c, kc), d, NT))
    stat_ref[0, 0:1] = top
    stat_ref[0, 1:2] = norm
    stat_ref[0, 2:3] = mix


def own_stats(kv, qd, kc=1024):
    _, pieces, nh, tok, _ = kv.shape
    own, width = pieces * tok, nh * HD
    return pl.pallas_call(
        functools.partial(own_stats_kernel, kc),
        grid=(nh,),
        out_shape=jax.ShapeDtypeStruct((nh, 8, own), F32),
        in_specs=[per_head(kv.shape), per_head(qd.shape)],
        out_specs=stat_block(own),
        scratch_shapes=[pltpu.VMEM((own, own), F32)],
        compiler_params=params(),
        cost_estimate=pl.CostEstimate(
            flops=4 * own * own * width, bytes_accessed=8 * own * width, transcendentals=own * own * nh
        ),
        name="own_stats",
    )(kv, qd)


def memory_kernel(kc, lists_ref, stat_ref, recv_ref, qd_ref, ret_ref, fin_ref, k_s, v_s):
    mem, own = k_s.shape[0], stat_ref.shape[2]
    count = lists_ref[mem // FBLK]
    load_memory(lists_ref, recv_ref, k_s, v_s)
    q, d = rows_of(qd_ref, 0, 0, own), rows_of(qd_ref, 1, 0, own)
    top_own = stat_ref[0, 0:1]
    top = top_own
    scores = []
    for c in range(0, mem, kc):
        s = dot(k_s[c : c + kc], q, NT)
        if c + kc > LEAST_LIVE * FBLK:
            s = masked(s, count, c)
        top = jnp.maximum(top, jnp.max(s, axis=0, keepdims=True))
        scores.append(s)
    shrink = jnp.exp2((top_own - top) * TO_EXP2)
    norm = stat_ref[0, 1:2] * shrink
    mix = stat_ref[0, 2:3] * shrink
    parts = []
    for i, s in enumerate(scores):
        e = jnp.exp2((s - top) * TO_EXP2)
        dp = dot(v_s[i * kc : (i + 1) * kc], d, NT)
        norm = norm + column_sum(e)
        mix = mix + column_sum(e * dp)
        parts.append((e, dp))
    inv = 1.0 / norm
    delta = mix * inv
    for i, (e, dp) in enumerate(parts):
        p = e * inv
        ds = (p * (dp - delta)).astype(BF16)
        gk = (dot(ds, q, NN) * SCALE).astype(BF16)
        gv = dot(p.astype(BF16), d, NN).astype(BF16)
        for j in range(kc // FBLK):
            rows = slice(j * FBLK, (j + 1) * FBLK)
            at = lists_ref[i * (kc // FBLK) + j]
            if (i + 1) * kc <= LEAST_LIVE * FBLK:
                ret_ref[at, 0] = gk[rows]
                ret_ref[at, 1] = gv[rows]
            else:

                @pl.when(i * (kc // FBLK) + j < count)
                def _():
                    ret_ref[at, 0] = gk[rows]
                    ret_ref[at, 1] = gv[rows]

    fin_ref[0, 0:1] = top
    fin_ref[0, 1:2] = inv
    fin_ref[0, 2:3] = delta


def memory(lists, stat, recv, qd, kc=128):
    mem = (lists.shape[0] - 1) * FBLK
    nh, _, own = stat.shape
    width = nh * HD
    return pl.pallas_call(
        functools.partial(memory_kernel, kc),
        grid=(nh,),
        out_shape=(
            pltpu.HBM(recv.shape, BF16),
            jax.ShapeDtypeStruct((nh, 8, own), F32),
        ),
        in_specs=[smem(), stat_block(own), per_head(recv.shape), per_head(qd.shape)],
        out_specs=(per_head(recv.shape), stat_block(own)),
        scratch_shapes=[pltpu.VMEM((mem, HD), BF16)] * 2,
        compiler_params=params(),
        cost_estimate=pl.CostEstimate(
            flops=8 * own * mem * width, bytes_accessed=8 * own * width, transcendentals=own * mem * nh
        ),
        name="memory",
    )(lists, stat, recv, qd)


def own_grads_kernel(kc, lists_ref, fin_ref, recv_ref, kv_ref, qd_ref, *refs):
    *dq_refs, own_ref, mk_s, mv_s = refs
    own, mem = fin_ref.shape[2], mk_s.shape[0]
    tok = own // len(dq_refs)
    load_memory(lists_ref, recv_ref, mk_s, mv_s)
    q, d = rows_of(qd_ref, 0, 0, own), rows_of(qd_ref, 1, 0, own)
    top, inv, delta = fin_ref[0, 0:1], fin_ref[0, 1:2], fin_ref[0, 2:3]

    def probabilities(k, v, count=None):
        s = dot(k, q, NT)
        if count is not None:
            s = masked(s, count)
        p = jnp.exp2((s - top) * TO_EXP2) * inv
        return p, (p * (dot(v, d, NT) - delta)).astype(BF16)

    _, ds = probabilities(mk_s[...], mv_s[...], lists_ref[mem // FBLK])
    dq = dot(ds, mk_s[...], TN)
    for c in range(0, own, kc):
        k, v = rows_of(kv_ref, 0, c, kc), rows_of(kv_ref, 1, c, kc)
        p, ds = probabilities(k, v)
        dq = dq + dot(ds, k, TN)
        own_ref[0, c : c + kc] = dot(ds, q, NN) * SCALE
        own_ref[1, c : c + kc] = dot(p.astype(BF16), d, NN)
    dq = (dq * SCALE).astype(BF16)
    for i, ref in enumerate(dq_refs):
        ref[0] = dq[i * tok : (i + 1) * tok]


def own_grads(lists, fin, recv, kv, qd, kc=1024):
    _, pieces, nh, tok, _ = kv.shape
    own, width = pieces * tok, nh * HD
    mem = (lists.shape[0] - 1) * FBLK
    total = own + mem
    piece, whole = (1, nh, tok, HD), (2, nh, own, HD)
    *dq, grads = pl.pallas_call(
        functools.partial(own_grads_kernel, kc),
        grid=(nh,),
        out_shape=[pltpu.HBM(piece, BF16)] * pieces + [pltpu.HBM(whole, F32)],
        in_specs=[smem(), stat_block(own), per_head(recv.shape), per_head(kv.shape), per_head(qd.shape)],
        out_specs=[per_head(piece)] * pieces + [per_head(whole)],
        scratch_shapes=[pltpu.VMEM((mem, HD), BF16)] * 2,
        compiler_params=params(),
        cost_estimate=pl.CostEstimate(
            flops=10 * own * total * width, bytes_accessed=16 * own * width, transcendentals=own * total * nh
        ),
        name="own_grads",
    )(lists, fin, recv, kv, qd)
    return dq, grads


def collect_kernel(blocks_ref, own_ref, back_ref, *refs):
    *out_refs, acc = refs
    slots = back_ref.shape[0]
    tok = acc.shape[1] // len(out_refs)
    acc[...] = own_ref[...]
    for s in range(slots):

        @pl.when(blocks_ref[slots + s] != 0)
        def _():
            rows = pl.ds(pl.multiple_of(blocks_ref[s] * FBLK, FBLK), FBLK)
            acc[:, rows, :] += back_ref[s].astype(F32)

    for i, ref in enumerate(out_refs):
        ref[...] = acc[:, i * tok : (i + 1) * tok, :].astype(BF16)


def collect(blocks, own, back, pieces):
    _, nh, rows, _ = own.shape
    piece = (2, nh, rows // pieces, HD)
    return pl.pallas_call(
        collect_kernel,
        grid=(nh,),
        out_shape=[jax.ShapeDtypeStruct(piece, BF16)] * pieces,
        in_specs=[smem(), per_head(own.shape), per_head(back.shape)],
        out_specs=[per_head(piece)] * pieces,
        scratch_shapes=[pltpu.VMEM((2, rows, HD), F32)],
        compiler_params=params(),
        name="collect",
    )(blocks, own, back)


def pick_kernel(blocks_ref, kv_ref, out_ref, sems):
    per = kv_ref.shape[3] // FBLK
    copies = []
    for s in range(out_ref.shape[0]):
        block = blocks_ref[s]
        rows = pl.ds(pl.multiple_of(lax.rem(block, per) * FBLK, FBLK), FBLK)
        copies.append(
            pltpu.make_async_copy(kv_ref.at[:, lax.div(block, per), :, rows, :], out_ref.at[s], sems.at[s])
        )
    for copy in copies:
        copy.start()
    for copy in copies:
        copy.wait()


def pick(blocks, kv, slots):
    _, _, nh, _, _ = kv.shape
    return pl.pallas_call(
        pick_kernel,
        out_shape=pltpu.HBM((slots, 2, nh, FBLK, HD), BF16),
        in_specs=[smem(), vmem()],
        out_specs=anywhere(),
        scratch_shapes=[pltpu.SemaphoreType.DMA((slots,))],
        compiler_params=pltpu.CompilerParams(vmem_limit_bytes=SMALL_LIMIT),
        name="pick",
    )(blocks, kv)


def cut_kernel(me_ref, a_ref, b_ref, *refs):
    *out_refs, wide, sems = refs
    count = len(out_refs)
    width = wide.shape[3]
    copies = []
    for k in range(count):
        columns = pl.ds(pl.multiple_of(lax.rem(me_ref[0] + k, count) * width, HD), width)
        for i, ref in enumerate((a_ref, b_ref)):
            copies.append(pltpu.make_async_copy(ref.at[:, columns], wide.at[k, i], sems.at[k, i]))
    for copy in copies:
        copy.start()
    for k, out_ref in enumerate(out_refs):
        for i in range(2):
            copies[2 * k + i].wait()
            for h in range(width // HD):
                out_ref[i, h] = wide[k, i, :, h * HD : (h + 1) * HD]


def cut(me, a, b, count):
    tok, width = a.shape
    width //= count
    return pl.pallas_call(
        cut_kernel,
        out_shape=[jax.ShapeDtypeStruct((2, width // HD, tok, HD), BF16)] * count,
        in_specs=[smem(), anywhere(), anywhere()],
        out_specs=[vmem()] * count,
        scratch_shapes=[pltpu.VMEM((count, 2, tok, width), BF16), pltpu.SemaphoreType.DMA((count, 2))],
        compiler_params=pltpu.CompilerParams(vmem_limit_bytes=MOST_VMEM),
        name="cut",
    )(me, a, b)


def place_kernel(count, me_ref, *refs):
    for k, ref in enumerate(refs[:count]):
        heads = ref.shape[1]
        of = lax.rem(me_ref[0] + k, count)
        for h in range(heads):
            columns = pl.ds(pl.multiple_of((of * heads + h) * HD, HD), HD)
            for i, out_ref in enumerate(refs[count:]):
                out_ref[:, columns] = ref[i, h]


def place(me, pieces):
    arrays, nh, tok, _ = pieces[0].shape
    count = len(pieces)
    return pl.pallas_call(
        functools.partial(place_kernel, count),
        out_shape=[jax.ShapeDtypeStruct((tok, nh * HD * count), BF16)] * arrays,
        in_specs=[smem()] + [vmem()] * count,
        out_specs=[vmem()] * arrays,
        compiler_params=pltpu.CompilerParams(vmem_limit_bytes=SMALL_LIMIT),
        name="place",
    )(me, *pieces)


def shift(parts, sign):
    n = len(parts)
    got = {0: parts[0]}
    for k in (1, 7, 2, 6, 3, 5, 4):
        got[k] = lax.ppermute(parts[k], "head", [(i, (i + sign * k) % n) for i in range(n)])
    return [got[k] for k in range(n)]


def body(query, key, value, out_grad, intersection, counts):
    frames, heads = lax.axis_size("tok"), lax.axis_size("head")
    frame, me = lax.axis_index("tok"), lax.axis_index("head")
    me1 = me[None]
    blk_tok = query.shape[0] // FBLK
    blk_dev = blk_tok * heads
    slots = jnp.arange(intersection.shape[1], dtype=jnp.int32)
    live = slots[None, :] < counts[:, None]
    safe = jnp.maximum(intersection, 0)
    mine = live & (safe // blk_dev == frame)
    wanted = jnp.any(mine, axis=1).astype(jnp.int32)
    block = jnp.sum(jnp.where(mine, safe % blk_dev, 0), axis=1)
    piece = (me - block // blk_tok + heads) % heads
    blocks = jnp.concatenate([piece * blk_tok + block % blk_tok, wanted])
    my_ids = lax.dynamic_index_in_dim(safe, frame, 0, keepdims=False) // blk_dev
    my_count = lax.dynamic_index_in_dim(counts, frame, 0, keepdims=True)
    lists = jnp.concatenate([my_ids, my_count])

    kv = jnp.stack(shift(cut(me1, key, value, heads), 1), axis=1)
    sent = pick(blocks, kv, frames)
    query, out_grad, sent = lax.optimization_barrier((query, out_grad, sent))
    recv = lax.all_to_all(sent, "tok", split_axis=0, concat_axis=0, tiled=True)
    qd = jnp.stack(shift(cut(me1, query, out_grad, heads), 1), axis=1)
    stat = own_stats(kv, qd)
    ret, fin = memory(lists, stat, recv, qd)
    back = lax.all_to_all(ret, "tok", split_axis=0, concat_axis=0, tiled=True)
    dq, own = own_grads(lists, fin, recv, kv, qd)
    (dq_out,) = place(me1, shift(dq, -1))
    back, dq_out = lax.optimization_barrier((back, dq_out))
    dk_out, dv_out = place(me1, shift(collect(blocks, own, back, heads), -1))
    return (dq_out, dk_out, dv_out)


def solution(mesh):
    rows = P(("tok", "head"), None)
    return jax.shard_map(
        body,
        mesh=mesh,
        in_specs=(rows, rows, rows, rows, P(), P()),
        out_specs=(rows, rows, rows),
        check_vma=False,
    )
```

```python
import functools
import math

import jax
import jax.numpy as jnp
from jax import lax
from jax.experimental import pallas as pl
from jax.experimental.pallas import tpu as pltpu
from jax.sharding import PartitionSpec as P

HD = 128
FBLK = 32
LEAST_LIVE = 12
SCALE = 1.0 / math.sqrt(HD)
TO_EXP2 = SCALE * math.log2(math.e)
VMEM_LIMIT = 40 * 2**20
MOST_VMEM = 60 * 2**20
SMALL_LIMIT = 16 * 2**20
NN = (((1,), (0,)), ((), ()))
NT = (((1,), (1,)), ((), ()))
TN = (((0,), (0,)), ((), ()))
F32 = jnp.float32
BF16 = jnp.bfloat16


def smem():
    return pl.BlockSpec(memory_space=pltpu.SMEM)


def anywhere():
    return pl.BlockSpec(memory_space=pl.ANY)


def per_head(shape):
    lead = len(shape) - 3
    return pl.BlockSpec((*shape[:lead], None, *shape[-2:]), lambda h: (0,) * lead + (h, 0, 0))


def vmem():
    return pl.BlockSpec(memory_space=pltpu.VMEM)


def array_of(shape, i):
    lead = len(shape) - 4
    return pl.BlockSpec((1, *shape[1 : 1 + lead], None, *shape[-2:]), lambda h: (i,) + (0,) * lead + (h, 0, 0))


def stat_block(own):
    return pl.BlockSpec((1, 8, own), lambda h: (h, 0, 0))


def params(limit=VMEM_LIMIT):
    return pltpu.CompilerParams(vmem_limit_bytes=limit, dimension_semantics=("arbitrary",))


def dot(a, b, dims):
    return lax.dot_general(a, b, dims, preferred_element_type=F32)


def column_sum(x):
    return jnp.sum(x, axis=0, keepdims=True)


def rows_of(ref, which, lo, count):
    tok = ref.shape[2]
    return ref[which, lo // tok : (lo + count) // tok].reshape(count, HD)


def load_memory(lists_ref, recv_ref, k_s, v_s):
    for j in range(k_s.shape[0] // FBLK):
        k_s[j * FBLK : (j + 1) * FBLK] = recv_ref[lists_ref[j], 0]
        v_s[j * FBLK : (j + 1) * FBLK] = recv_ref[lists_ref[j], 1]


def masked(s, count, first=0):
    row = lax.broadcasted_iota(jnp.int32, s.shape, 0)
    return jnp.where(row < count * FBLK - first, s, -jnp.inf)


def own_stats_kernel(kc, kv_ref, qd_ref, stat_ref, s_s):
    own = s_s.shape[0]
    q, d = rows_of(qd_ref, 0, 0, own), rows_of(qd_ref, 1, 0, own)
    top = jnp.full((1, own), -jnp.inf, F32)
    for c in range(0, own, kc):
        s = dot(rows_of(kv_ref, 0, c, kc), q, NT)
        s_s[c : c + kc] = s
        top = jnp.maximum(top, jnp.max(s, axis=0, keepdims=True))
    norm = jnp.zeros((1, own), F32)
    mix = jnp.zeros((1, own), F32)
    for c in range(0, own, kc):
        e = jnp.exp2((s_s[c : c + kc] - top) * TO_EXP2)
        norm = norm + column_sum(e)
        mix = mix + column_sum(e * dot(rows_of(kv_ref, 1, c, kc), d, NT))
    stat_ref[0, 0:1] = top
    stat_ref[0, 1:2] = norm
    stat_ref[0, 2:3] = mix


def own_stats(kv, qd, kc=1024):
    _, pieces, nh, tok, _ = kv.shape
    own, width = pieces * tok, nh * HD
    return pl.pallas_call(
        functools.partial(own_stats_kernel, kc),
        grid=(nh,),
        out_shape=jax.ShapeDtypeStruct((nh, 8, own), F32),
        in_specs=[per_head(kv.shape), per_head(qd.shape)],
        out_specs=stat_block(own),
        scratch_shapes=[pltpu.VMEM((own, own), F32)],
        compiler_params=params(),
        cost_estimate=pl.CostEstimate(
            flops=4 * own * own * width, bytes_accessed=8 * own * width, transcendentals=own * own * nh
        ),
        name="own_stats",
    )(kv, qd)


def memory_kernel(tq, lists_ref, stat_ref, recv_ref, q_ref, d_ref, ret_ref, fin_ref, k_s, v_s, g_s):
    mem, own = k_s.shape[0], stat_ref.shape[2]
    memd = mem // FBLK
    count = lists_ref[memd]
    sure = LEAST_LIVE * FBLK
    load_memory(lists_ref, recv_ref, k_s, v_s)

    def products(t):
        q, d = rows_of(q_ref, 0, t, tq), rows_of(d_ref, 0, t, tq)
        s, dp = dot(k_s[...], q, NT), dot(v_s[...], d, NT)
        return q, d, jnp.concatenate([s[:sure], masked(s[sure:], count, sure)]), dp

    def terms(t, q, d, s, dp):
        qs = slice(t, t + tq)
        top_own = stat_ref[0, 0:1, qs]
        top = jnp.maximum(top_own, jnp.max(s, axis=0, keepdims=True))
        shrink = jnp.exp2((top_own - top) * TO_EXP2)
        e = jnp.exp2((s - top) * TO_EXP2)
        inv = 1.0 / (stat_ref[0, 1:2, qs] * shrink + column_sum(e))
        delta = (stat_ref[0, 2:3, qs] * shrink + column_sum(e * dp)) * inv
        fin_ref[0, 0:1, qs] = top
        fin_ref[0, 1:2, qs] = inv
        fin_ref[0, 2:3, qs] = delta
        p = e * inv
        gk = dot((p * (dp - delta)).astype(BF16), q, NN)
        gv = dot(p.astype(BF16), d, NN)
        g_s[0] = gk if t == 0 else g_s[0] + gk
        g_s[1] = gv if t == 0 else g_s[1] + gv

    ahead = products(0)
    for t in range(0, own, tq):
        now = ahead
        if t + tq < own:
            ahead = products(t + tq)
        terms(t, *now)
    for j in range(memd):
        rows = slice(j * FBLK, (j + 1) * FBLK)

        @pl.when(j < count)
        def _():
            ret_ref[lists_ref[j], 0] = (g_s[0, rows] * SCALE).astype(BF16)
            ret_ref[lists_ref[j], 1] = g_s[1, rows].astype(BF16)


def memory(lists, stat, recv, qd, tq=512):
    mem = (lists.shape[0] - 1) * FBLK
    nh, _, own = stat.shape
    width = nh * HD
    return pl.pallas_call(
        functools.partial(memory_kernel, tq),
        grid=(nh,),
        out_shape=(
            pltpu.HBM(recv.shape, BF16),
            jax.ShapeDtypeStruct((nh, 8, own), F32),
        ),
        in_specs=[smem(), stat_block(own), per_head(recv.shape), array_of(qd.shape, 0), array_of(qd.shape, 1)],
        out_specs=(per_head(recv.shape), stat_block(own)),
        scratch_shapes=[pltpu.VMEM((mem, HD), BF16)] * 2 + [pltpu.VMEM((2, mem, HD), F32)],
        compiler_params=params(MOST_VMEM),
        cost_estimate=pl.CostEstimate(
            flops=8 * own * mem * width, bytes_accessed=8 * own * width, transcendentals=own * mem * nh
        ),
        name="memory",
    )(lists, stat, recv, qd, qd)


def own_grads_kernel(kc, lists_ref, fin_ref, recv_ref, kv_ref, qd_ref, *refs):
    *dq_refs, own_ref, mk_s, mv_s = refs
    own, mem = fin_ref.shape[2], mk_s.shape[0]
    tok = own // len(dq_refs)
    load_memory(lists_ref, recv_ref, mk_s, mv_s)
    q, d = rows_of(qd_ref, 0, 0, own), rows_of(qd_ref, 1, 0, own)
    top, inv, delta = fin_ref[0, 0:1], fin_ref[0, 1:2], fin_ref[0, 2:3]

    def probabilities(k, v, count=None):
        s = dot(k, q, NT)
        if count is not None:
            s = masked(s, count)
        p = jnp.exp2((s - top) * TO_EXP2) * inv
        return p, (p * (dot(v, d, NT) - delta)).astype(BF16)

    _, ds = probabilities(mk_s[...], mv_s[...], lists_ref[mem // FBLK])
    dq = dot(ds, mk_s[...], TN)
    for c in range(0, own, kc):
        k, v = rows_of(kv_ref, 0, c, kc), rows_of(kv_ref, 1, c, kc)
        p, ds = probabilities(k, v)
        dq = dq + dot(ds, k, TN)
        own_ref[0, c : c + kc] = dot(ds, q, NN) * SCALE
        own_ref[1, c : c + kc] = dot(p.astype(BF16), d, NN)
    dq = (dq * SCALE).astype(BF16)
    for i, ref in enumerate(dq_refs):
        ref[0] = dq[i * tok : (i + 1) * tok]


def own_grads(lists, fin, recv, kv, qd, kc=1024):
    _, pieces, nh, tok, _ = kv.shape
    own, width = pieces * tok, nh * HD
    mem = (lists.shape[0] - 1) * FBLK
    total = own + mem
    piece, whole = (1, nh, tok, HD), (2, nh, own, HD)
    *dq, grads = pl.pallas_call(
        functools.partial(own_grads_kernel, kc),
        grid=(nh,),
        out_shape=[pltpu.HBM(piece, BF16)] * pieces + [pltpu.HBM(whole, F32)],
        in_specs=[smem(), stat_block(own), per_head(recv.shape), per_head(kv.shape), per_head(qd.shape)],
        out_specs=[per_head(piece)] * pieces + [per_head(whole)],
        scratch_shapes=[pltpu.VMEM((mem, HD), BF16)] * 2,
        compiler_params=params(),
        cost_estimate=pl.CostEstimate(
            flops=10 * own * total * width, bytes_accessed=16 * own * width, transcendentals=own * total * nh
        ),
        name="own_grads",
    )(lists, fin, recv, kv, qd)
    return dq, grads


def collect_kernel(blocks_ref, own_ref, back_ref, *refs):
    *out_refs, acc = refs
    slots = back_ref.shape[0]
    tok = acc.shape[2] // len(out_refs)
    acc[...] = own_ref[...]
    for s in range(slots):

        @pl.when(blocks_ref[slots + s] != 0)
        def _():
            rows = pl.ds(pl.multiple_of(blocks_ref[s] * FBLK, FBLK), FBLK)
            acc[:, :, rows, :] += back_ref[s].astype(F32)

    for i, ref in enumerate(out_refs):
        ref[...] = acc[:, :, i * tok : (i + 1) * tok, :].astype(BF16)


def collect(blocks, own, back, pieces):
    _, nh, rows, _ = own.shape
    piece = (2, nh, rows // pieces, HD)
    return pl.pallas_call(
        collect_kernel,
        out_shape=[jax.ShapeDtypeStruct(piece, BF16)] * pieces,
        in_specs=[smem(), vmem(), vmem()],
        out_specs=[vmem()] * pieces,
        scratch_shapes=[pltpu.VMEM(own.shape, F32)],
        compiler_params=pltpu.CompilerParams(vmem_limit_bytes=SMALL_LIMIT),
        name="collect",
    )(blocks, own, back)


def pick_kernel(blocks_ref, kv_ref, out_ref, sems):
    per = kv_ref.shape[3] // FBLK
    copies = []
    for s in range(out_ref.shape[0]):
        block = blocks_ref[s]
        rows = pl.ds(pl.multiple_of(lax.rem(block, per) * FBLK, FBLK), FBLK)
        copies.append(
            pltpu.make_async_copy(kv_ref.at[:, lax.div(block, per), :, rows, :], out_ref.at[s], sems.at[s])
        )
    for copy in copies:
        copy.start()
    for copy in copies:
        copy.wait()


def pick(blocks, kv, slots):
    _, _, nh, _, _ = kv.shape
    return pl.pallas_call(
        pick_kernel,
        out_shape=pltpu.HBM((slots, 2, nh, FBLK, HD), BF16),
        in_specs=[smem(), vmem()],
        out_specs=anywhere(),
        scratch_shapes=[pltpu.SemaphoreType.DMA((slots,))],
        compiler_params=pltpu.CompilerParams(vmem_limit_bytes=SMALL_LIMIT),
        name="pick",
    )(blocks, kv)


def cut_kernel(me_ref, a_ref, b_ref, *refs):
    *out_refs, wide, sems = refs
    count = len(out_refs)
    width = wide.shape[3]
    copies = []
    for k in range(count):
        columns = pl.ds(pl.multiple_of(lax.rem(me_ref[0] + k, count) * width, HD), width)
        for i, ref in enumerate((a_ref, b_ref)):
            copies.append(pltpu.make_async_copy(ref.at[:, columns], wide.at[k, i], sems.at[k, i]))
    for copy in copies:
        copy.start()
    for k, out_ref in enumerate(out_refs):
        for i in range(2):
            copies[2 * k + i].wait()
            for h in range(width // HD):
                out_ref[i, h] = wide[k, i, :, h * HD : (h + 1) * HD]


def cut(me, a, b, count):
    tok, width = a.shape
    width //= count
    return pl.pallas_call(
        cut_kernel,
        out_shape=[jax.ShapeDtypeStruct((2, width // HD, tok, HD), BF16)] * count,
        in_specs=[smem(), anywhere(), anywhere()],
        out_specs=[vmem()] * count,
        scratch_shapes=[pltpu.VMEM((count, 2, tok, width), BF16), pltpu.SemaphoreType.DMA((count, 2))],
        compiler_params=pltpu.CompilerParams(vmem_limit_bytes=MOST_VMEM),
        name="cut",
    )(me, a, b)


def place_kernel(count, me_ref, *refs):
    out_refs, sems = refs[count:-1], refs[-1]
    copies = []
    for k, ref in enumerate(refs[:count]):
        heads = ref.shape[1]
        of = lax.rem(me_ref[0] + k, count)
        for h in range(heads):
            columns = pl.ds(pl.multiple_of((of * heads + h) * HD, HD), HD)
            for i, out_ref in enumerate(out_refs):
                copies.append(pltpu.make_async_copy(ref.at[i, h], out_ref.at[:, columns], sems.at[i, k, h]))
    for copy in copies:
        copy.start()
    for copy in copies:
        copy.wait()


def place(me, pieces):
    arrays, nh, tok, _ = pieces[0].shape
    count = len(pieces)
    return pl.pallas_call(
        functools.partial(place_kernel, count),
        out_shape=[pltpu.HBM((tok, nh * HD * count), BF16)] * arrays,
        in_specs=[smem()] + [vmem()] * count,
        out_specs=[anywhere()] * arrays,
        scratch_shapes=[pltpu.SemaphoreType.DMA((arrays, count, nh))],
        compiler_params=pltpu.CompilerParams(vmem_limit_bytes=SMALL_LIMIT),
        name="place",
    )(me, *pieces)


def shift(parts, sign):
    n = len(parts)
    got = {0: parts[0]}
    for k in (1, 7, 2, 6, 3, 5, 4):
        got[k] = lax.ppermute(parts[k], "head", [(i, (i + sign * k) % n) for i in range(n)])
    return [got[k] for k in range(n)]


def body(query, key, value, out_grad, intersection, counts):
    frames, heads = lax.axis_size("tok"), lax.axis_size("head")
    frame, me = lax.axis_index("tok"), lax.axis_index("head")
    me1 = me[None]
    blk_tok = query.shape[0] // FBLK
    blk_dev = blk_tok * heads
    slots = jnp.arange(intersection.shape[1], dtype=jnp.int32)
    live = slots[None, :] < counts[:, None]
    safe = jnp.maximum(intersection, 0)
    mine = live & (safe // blk_dev == frame)
    wanted = jnp.any(mine, axis=1).astype(jnp.int32)
    block = jnp.sum(jnp.where(mine, safe % blk_dev, 0), axis=1)
    piece = (me - block // blk_tok + heads) % heads
    blocks = jnp.concatenate([piece * blk_tok + block % blk_tok, wanted])
    my_ids = lax.dynamic_index_in_dim(safe, frame, 0, keepdims=False) // blk_dev
    my_count = lax.dynamic_index_in_dim(counts, frame, 0, keepdims=True)
    lists = jnp.concatenate([my_ids, my_count])

    kv = jnp.stack(shift(cut(me1, key, value, heads), 1), axis=1)
    sent = pick(blocks, kv, frames)
    query, out_grad, sent = lax.optimization_barrier((query, out_grad, sent))
    recv = lax.all_to_all(sent, "tok", split_axis=0, concat_axis=0, tiled=True)
    qd = jnp.stack(shift(cut(me1, query, out_grad, heads), 1), axis=1)
    stat = own_stats(kv, qd)
    ret, fin = memory(lists, stat, recv, qd)
    back = lax.all_to_all(ret, "tok", split_axis=0, concat_axis=0, tiled=True)
    dq, own = own_grads(lists, fin, recv, kv, qd)
    (dq_out,) = place(me1, shift(dq, -1))
    back, dq_out = lax.optimization_barrier((back, dq_out))
    dk_out, dv_out = place(me1, shift(collect(blocks, own, back, heads), -1))
    return (dq_out, dk_out, dv_out)


def solution(mesh):
    rows = P(("tok", "head"), None)
    return jax.shard_map(
        body,
        mesh=mesh,
        in_specs=(rows, rows, rows, rows, P(), P()),
        out_specs=(rows, rows, rows),
        check_vma=False,
    )
```

```python
import functools
import math

import jax
import jax.numpy as jnp
from jax import lax
from jax.experimental import pallas as pl
from jax.experimental.pallas import tpu as pltpu
from jax.sharding import PartitionSpec as P

HD = 128
FBLK = 32
LEAST_LIVE = 12
ORDER = (1, 7, 2, 6, 3, 5, 4)
SCALE = 1.0 / math.sqrt(HD)
TO_EXP2 = SCALE * math.log2(math.e)
VMEM_LIMIT = 40 * 2**20
MOST_VMEM = 60 * 2**20
SMALL_LIMIT = 16 * 2**20
NN = (((1,), (0,)), ((), ()))
NT = (((1,), (1,)), ((), ()))
TN = (((0,), (0,)), ((), ()))
F32 = jnp.float32
BF16 = jnp.bfloat16


def smem():
    return pl.BlockSpec(memory_space=pltpu.SMEM)


def anywhere():
    return pl.BlockSpec(memory_space=pl.ANY)


def per_head(shape):
    lead = len(shape) - 3
    return pl.BlockSpec((*shape[:lead], None, *shape[-2:]), lambda h: (0,) * lead + (h, 0, 0))


def vmem():
    return pl.BlockSpec(memory_space=pltpu.VMEM)


def array_of(shape, i):
    lead = len(shape) - 4
    return pl.BlockSpec((1, *shape[1 : 1 + lead], None, *shape[-2:]), lambda h: (i,) + (0,) * lead + (h, 0, 0))


def stat_block(own):
    return pl.BlockSpec((1, 8, own), lambda h: (h, 0, 0))


def params(limit=VMEM_LIMIT):
    return pltpu.CompilerParams(vmem_limit_bytes=limit, dimension_semantics=("arbitrary",))


def dot(a, b, dims):
    return lax.dot_general(a, b, dims, preferred_element_type=F32)


def column_sum(x):
    return jnp.sum(x, axis=0, keepdims=True)


def rows_of(ref, which, lo, count):
    tok = ref.shape[2]
    return ref[which, lo // tok : (lo + count) // tok].reshape(count, HD)


def load_memory(lists_ref, recv_ref, k_s, v_s):
    for j in range(k_s.shape[0] // FBLK):
        k_s[j * FBLK : (j + 1) * FBLK] = recv_ref[lists_ref[j], 0]
        v_s[j * FBLK : (j + 1) * FBLK] = recv_ref[lists_ref[j], 1]


def masked(s, count, first=0):
    row = lax.broadcasted_iota(jnp.int32, s.shape, 0)
    return jnp.where(row < count * FBLK - first, s, -jnp.inf)


def own_stats_kernel(kc, kv_ref, qd_ref, stat_ref, s_s):
    own = s_s.shape[0]
    q, d = rows_of(qd_ref, 0, 0, own), rows_of(qd_ref, 1, 0, own)
    top = jnp.full((1, own), -jnp.inf, F32)
    for c in range(0, own, kc):
        s = dot(rows_of(kv_ref, 0, c, kc), q, NT)
        s_s[c : c + kc] = s
        top = jnp.maximum(top, jnp.max(s, axis=0, keepdims=True))
    norm = jnp.zeros((1, own), F32)
    mix = jnp.zeros((1, own), F32)
    for c in range(0, own, kc):
        e = jnp.exp2((s_s[c : c + kc] - top) * TO_EXP2)
        norm = norm + column_sum(e)
        mix = mix + column_sum(e * dot(rows_of(kv_ref, 1, c, kc), d, NT))
    stat_ref[0, 0:1] = top
    stat_ref[0, 1:2] = norm
    stat_ref[0, 2:3] = mix


def own_stats(kv, qd, kc=1024):
    _, pieces, nh, tok, _ = kv.shape
    own, width = pieces * tok, nh * HD
    return pl.pallas_call(
        functools.partial(own_stats_kernel, kc),
        grid=(nh,),
        out_shape=jax.ShapeDtypeStruct((nh, 8, own), F32),
        in_specs=[per_head(kv.shape), per_head(qd.shape)],
        out_specs=stat_block(own),
        scratch_shapes=[pltpu.VMEM((own, own), F32)],
        compiler_params=params(),
        cost_estimate=pl.CostEstimate(
            flops=4 * own * own * width, bytes_accessed=8 * own * width, transcendentals=own * own * nh
        ),
        name="own_stats",
    )(kv, qd)


def memory_kernel(tq, lists_ref, stat_ref, recv_ref, q_ref, d_ref, ret_ref, fin_ref, k_s, v_s, g_s):
    mem, own = k_s.shape[0], stat_ref.shape[2]
    memd = mem // FBLK
    count = lists_ref[memd]
    sure = LEAST_LIVE * FBLK
    load_memory(lists_ref, recv_ref, k_s, v_s)

    def products(t):
        q, d = rows_of(q_ref, 0, t, tq), rows_of(d_ref, 0, t, tq)
        s, dp = dot(k_s[...], q, NT), dot(v_s[...], d, NT)
        return q, d, jnp.concatenate([s[:sure], masked(s[sure:], count, sure)]), dp

    def terms(t, q, d, s, dp):
        qs = slice(t, t + tq)
        top_own = stat_ref[0, 0:1, qs]
        top = jnp.maximum(top_own, jnp.max(s, axis=0, keepdims=True))
        shrink = jnp.exp2((top_own - top) * TO_EXP2)
        e = jnp.exp2((s - top) * TO_EXP2)
        inv = 1.0 / (stat_ref[0, 1:2, qs] * shrink + column_sum(e))
        delta = (stat_ref[0, 2:3, qs] * shrink + column_sum(e * dp)) * inv
        fin_ref[0, 0:1, qs] = top
        fin_ref[0, 1:2, qs] = inv
        fin_ref[0, 2:3, qs] = delta
        p = e * inv
        gk = dot((p * (dp - delta)).astype(BF16), q, NN)
        gv = dot(p.astype(BF16), d, NN)
        g_s[0] = gk if t == 0 else g_s[0] + gk
        g_s[1] = gv if t == 0 else g_s[1] + gv

    ahead = products(0)
    for t in range(0, own, tq):
        now = ahead
        if t + tq < own:
            ahead = products(t + tq)
        terms(t, *now)
    for j in range(memd):
        rows = slice(j * FBLK, (j + 1) * FBLK)

        @pl.when(j < count)
        def _():
            ret_ref[lists_ref[j], 0] = (g_s[0, rows] * SCALE).astype(BF16)
            ret_ref[lists_ref[j], 1] = g_s[1, rows].astype(BF16)


def memory(lists, stat, recv, qd, tq=512):
    mem = (lists.shape[0] - 1) * FBLK
    nh, _, own = stat.shape
    width = nh * HD
    return pl.pallas_call(
        functools.partial(memory_kernel, tq),
        grid=(nh,),
        out_shape=(
            pltpu.HBM(recv.shape, BF16),
            jax.ShapeDtypeStruct((nh, 8, own), F32),
        ),
        in_specs=[smem(), stat_block(own), per_head(recv.shape), array_of(qd.shape, 0), array_of(qd.shape, 1)],
        out_specs=(per_head(recv.shape), stat_block(own)),
        scratch_shapes=[pltpu.VMEM((mem, HD), BF16)] * 2 + [pltpu.VMEM((2, mem, HD), F32)],
        compiler_params=params(MOST_VMEM),
        cost_estimate=pl.CostEstimate(
            flops=8 * own * mem * width, bytes_accessed=8 * own * width, transcendentals=own * mem * nh
        ),
        name="memory",
    )(lists, stat, recv, qd, qd)


def own_grads_kernel(kc, lists_ref, fin_ref, recv_ref, kv_ref, qd_ref, *refs):
    *dq_refs, own_ref, mk_s, mv_s = refs
    own, mem = fin_ref.shape[2], mk_s.shape[0]
    tok = own // len(dq_refs)
    load_memory(lists_ref, recv_ref, mk_s, mv_s)
    q, d = rows_of(qd_ref, 0, 0, own), rows_of(qd_ref, 1, 0, own)
    top, inv, delta = fin_ref[0, 0:1], fin_ref[0, 1:2], fin_ref[0, 2:3]

    def probabilities(k, v, count=None):
        s = dot(k, q, NT)
        if count is not None:
            s = masked(s, count)
        p = jnp.exp2((s - top) * TO_EXP2) * inv
        return p, (p * (dot(v, d, NT) - delta)).astype(BF16)

    _, ds = probabilities(mk_s[...], mv_s[...], lists_ref[mem // FBLK])
    dq = dot(ds, mk_s[...], TN)
    for c in range(0, own, kc):
        k, v = rows_of(kv_ref, 0, c, kc), rows_of(kv_ref, 1, c, kc)
        p, ds = probabilities(k, v)
        dq = dq + dot(ds, k, TN)
        own_ref[0, c : c + kc] = dot(ds, q, NN) * SCALE
        own_ref[1, c : c + kc] = dot(p.astype(BF16), d, NN)
    dq = (dq * SCALE).astype(BF16)
    for i, ref in enumerate(dq_refs):
        ref[0] = dq[i * tok : (i + 1) * tok]


def own_grads(lists, fin, recv, kv, qd, kc=1024):
    _, pieces, nh, tok, _ = kv.shape
    own, width = pieces * tok, nh * HD
    mem = (lists.shape[0] - 1) * FBLK
    total = own + mem
    piece, whole = (1, nh, tok, HD), (2, nh, own, HD)
    *dq, grads = pl.pallas_call(
        functools.partial(own_grads_kernel, kc),
        grid=(nh,),
        out_shape=[pltpu.HBM(piece, BF16)] * pieces + [pltpu.HBM(whole, F32)],
        in_specs=[smem(), stat_block(own), per_head(recv.shape), per_head(kv.shape), per_head(qd.shape)],
        out_specs=[per_head(piece)] * pieces + [per_head(whole)],
        scratch_shapes=[pltpu.VMEM((mem, HD), BF16)] * 2,
        compiler_params=params(),
        cost_estimate=pl.CostEstimate(
            flops=10 * own * total * width, bytes_accessed=16 * own * width, transcendentals=own * total * nh
        ),
        name="own_grads",
    )(lists, fin, recv, kv, qd)
    return dq, grads


def collect_kernel(blocks_ref, own_ref, back_ref, *refs):
    *out_refs, acc = refs
    slots = back_ref.shape[0]
    tok = acc.shape[2] // len(out_refs)
    acc[...] = own_ref[...]
    for s in range(slots):

        @pl.when(blocks_ref[slots + s] != 0)
        def _():
            rows = pl.ds(pl.multiple_of(blocks_ref[s] * FBLK, FBLK), FBLK)
            acc[:, :, rows, :] += back_ref[s].astype(F32)

    for i, ref in enumerate(out_refs):
        ref[...] = acc[:, :, i * tok : (i + 1) * tok, :].astype(BF16)


def collect(blocks, own, back, pieces):
    _, nh, rows, _ = own.shape
    piece = (2, nh, rows // pieces, HD)
    return pl.pallas_call(
        collect_kernel,
        out_shape=[jax.ShapeDtypeStruct(piece, BF16)] * pieces,
        in_specs=[smem(), vmem(), vmem()],
        out_specs=[vmem()] * pieces,
        scratch_shapes=[pltpu.VMEM(own.shape, F32)],
        compiler_params=pltpu.CompilerParams(vmem_limit_bytes=SMALL_LIMIT),
        name="collect",
    )(blocks, own, back)


def pick_kernel(blocks_ref, kv_ref, out_ref, sems):
    per = kv_ref.shape[3] // FBLK
    copies = []
    for s in range(out_ref.shape[0]):
        block = blocks_ref[s]
        rows = pl.ds(pl.multiple_of(lax.rem(block, per) * FBLK, FBLK), FBLK)
        copies.append(
            pltpu.make_async_copy(kv_ref.at[:, lax.div(block, per), :, rows, :], out_ref.at[s], sems.at[s])
        )
    for copy in copies:
        copy.start()
    for copy in copies:
        copy.wait()


def pick(blocks, kv, slots):
    _, _, nh, _, _ = kv.shape
    return pl.pallas_call(
        pick_kernel,
        out_shape=pltpu.HBM((slots, 2, nh, FBLK, HD), BF16),
        in_specs=[smem(), vmem()],
        out_specs=anywhere(),
        scratch_shapes=[pltpu.SemaphoreType.DMA((slots,))],
        compiler_params=pltpu.CompilerParams(vmem_limit_bytes=SMALL_LIMIT),
        name="pick",
    )(blocks, kv)


def cut_kernel(me_ref, a_ref, b_ref, *refs):
    *out_refs, sems = refs
    count = len(out_refs)
    copies = []
    for k in (*ORDER, 0):
        heads = out_refs[k].shape[1]
        to = lax.rem(me_ref[0] + k, count)
        for h in range(heads):
            columns = pl.ds(pl.multiple_of((to * heads + h) * HD, HD), HD)
            for i, ref in enumerate((a_ref, b_ref)):
                copies.append(pltpu.make_async_copy(ref.at[:, columns], out_refs[k].at[i, h], sems.at[i, k, h]))
    for copy in copies:
        copy.start()
    for copy in copies:
        copy.wait()


def cut(me, a, b, count):
    tok, width = a.shape
    nh = width // count // HD
    return pl.pallas_call(
        cut_kernel,
        out_shape=[jax.ShapeDtypeStruct((2, nh, tok, HD), BF16)] * count,
        in_specs=[smem(), anywhere(), anywhere()],
        out_specs=[vmem()] * count,
        scratch_shapes=[pltpu.SemaphoreType.DMA((2, count, nh))],
        compiler_params=pltpu.CompilerParams(vmem_limit_bytes=MOST_VMEM),
        name="cut",
    )(me, a, b)


def place_kernel(ks, count, arrays, me_ref, *refs):
    out_refs, sems = refs[-1 - arrays : -1], refs[-1]
    copies = []
    for n, (k, ref) in enumerate(zip(ks, refs)):
        heads = ref.shape[1]
        of = lax.rem(me_ref[0] + k, count)
        for h in range(heads):
            columns = pl.ds(pl.multiple_of((of * heads + h) * HD, HD), HD)
            for i, out_ref in enumerate(out_refs):
                copies.append(pltpu.make_async_copy(ref.at[i, h], out_ref.at[:, columns], sems.at[i, n, h]))
    for copy in copies:
        copy.start()
    for copy in copies:
        copy.wait()


def place_some(me, pieces, ks, before):
    arrays, nh, tok, _ = pieces[0].shape
    count = len(pieces)
    return pl.pallas_call(
        functools.partial(place_kernel, ks, count, arrays),
        out_shape=[pltpu.HBM((tok, nh * HD * count), BF16)] * arrays,
        in_specs=[smem()] + [vmem()] * len(ks) + [anywhere()] * len(before),
        out_specs=[anywhere()] * arrays,
        input_output_aliases={1 + len(ks) + i: i for i in range(len(before))},
        scratch_shapes=[pltpu.SemaphoreType.DMA((arrays, len(ks), nh))],
        compiler_params=pltpu.CompilerParams(vmem_limit_bytes=SMALL_LIMIT),
        name="place",
    )(me, *(pieces[k] for k in ks), *before)


def place(me, pieces):
    early = (0, *ORDER[:-2])
    return place_some(me, pieces, ORDER[-2:], place_some(me, pieces, early, ()))


def shift(parts, sign):
    n = len(parts)
    got = {0: parts[0]}
    for k in ORDER:
        got[k] = lax.ppermute(parts[k], "head", [(i, (i + sign * k) % n) for i in range(n)])
    return [got[k] for k in range(n)]


def body(query, key, value, out_grad, intersection, counts):
    frames, heads = lax.axis_size("tok"), lax.axis_size("head")
    frame, me = lax.axis_index("tok"), lax.axis_index("head")
    me1 = me[None]
    blk_tok = query.shape[0] // FBLK
    blk_dev = blk_tok * heads
    slots = jnp.arange(intersection.shape[1], dtype=jnp.int32)
    live = slots[None, :] < counts[:, None]
    safe = jnp.maximum(intersection, 0)
    mine = live & (safe // blk_dev == frame)
    wanted = jnp.any(mine, axis=1).astype(jnp.int32)
    block = jnp.sum(jnp.where(mine, safe % blk_dev, 0), axis=1)
    piece = (me - block // blk_tok + heads) % heads
    blocks = jnp.concatenate([piece * blk_tok + block % blk_tok, wanted])
    my_ids = lax.dynamic_index_in_dim(safe, frame, 0, keepdims=False) // blk_dev
    my_count = lax.dynamic_index_in_dim(counts, frame, 0, keepdims=True)
    lists = jnp.concatenate([my_ids, my_count])

    kv = jnp.stack(shift(cut(me1, key, value, heads), 1), axis=1)
    sent = pick(blocks, kv, frames)
    query, out_grad, sent = lax.optimization_barrier((query, out_grad, sent))
    recv = lax.all_to_all(sent, "tok", split_axis=0, concat_axis=0, tiled=True)
    qd = jnp.stack(shift(cut(me1, query, out_grad, heads), 1), axis=1)
    stat = own_stats(kv, qd)
    ret, fin = memory(lists, stat, recv, qd)
    back = lax.all_to_all(ret, "tok", split_axis=0, concat_axis=0, tiled=True)
    dq, own = own_grads(lists, fin, recv, kv, qd)
    (dq_out,) = place(me1, shift(dq, -1))
    back, dq_out = lax.optimization_barrier((back, dq_out))
    dk_out, dv_out = place(me1, shift(collect(blocks, own, back, heads), -1))
    return (dq_out, dk_out, dv_out)


def solution(mesh):
    rows = P(("tok", "head"), None)
    return jax.shard_map(
        body,
        mesh=mesh,
        in_specs=(rows, rows, rows, rows, P(), P()),
        out_specs=(rows, rows, rows),
        check_vma=False,
    )
```

```python
import functools
import math

import jax
import jax.numpy as jnp
from jax import lax
from jax.experimental import pallas as pl
from jax.experimental.pallas import tpu as pltpu
from jax.sharding import PartitionSpec as P

HD = 128
FBLK = 32
LEAST_LIVE = 12
ORDER = (1, 7, 2, 6, 3, 5, 4)
SCALE = 1.0 / math.sqrt(HD)
TO_EXP2 = SCALE * math.log2(math.e)
VMEM_LIMIT = 40 * 2**20
MOST_VMEM = 60 * 2**20
SMALL_LIMIT = 16 * 2**20
NN = (((1,), (0,)), ((), ()))
NT = (((1,), (1,)), ((), ()))
TN = (((0,), (0,)), ((), ()))
F32 = jnp.float32
BF16 = jnp.bfloat16


def smem():
    return pl.BlockSpec(memory_space=pltpu.SMEM)


def anywhere():
    return pl.BlockSpec(memory_space=pl.ANY)


def per_head(shape):
    lead = len(shape) - 3
    return pl.BlockSpec((*shape[:lead], None, *shape[-2:]), lambda h: (0,) * lead + (h, 0, 0))


def vmem():
    return pl.BlockSpec(memory_space=pltpu.VMEM)


def array_of(shape, i):
    lead = len(shape) - 4
    return pl.BlockSpec((1, *shape[1 : 1 + lead], None, *shape[-2:]), lambda h: (i,) + (0,) * lead + (h, 0, 0))


def stat_block(own):
    return pl.BlockSpec((1, 8, own), lambda h: (h, 0, 0))


def params(limit=VMEM_LIMIT):
    return pltpu.CompilerParams(vmem_limit_bytes=limit, dimension_semantics=("arbitrary",))


def dot(a, b, dims):
    return lax.dot_general(a, b, dims, preferred_element_type=F32)


def column_sum(x):
    return jnp.sum(x, axis=0, keepdims=True)


def rows_of(ref, which, lo, count):
    tok = ref.shape[2]
    return ref[which, lo // tok : (lo + count) // tok].reshape(count, HD)


def load_memory(lists_ref, recv_ref, k_s, v_s):
    for j in range(k_s.shape[0] // FBLK):
        k_s[j * FBLK : (j + 1) * FBLK] = recv_ref[lists_ref[j], 0]
        v_s[j * FBLK : (j + 1) * FBLK] = recv_ref[lists_ref[j], 1]


def masked(s, count, first=0):
    row = lax.broadcasted_iota(jnp.int32, s.shape, 0)
    return jnp.where(row < count * FBLK - first, s, -jnp.inf)


def own_stats_kernel(kc, kv_ref, qd_ref, stat_ref, s_s):
    own = s_s.shape[0]
    q, d = rows_of(qd_ref, 0, 0, own), rows_of(qd_ref, 1, 0, own)
    top = jnp.full((1, own), -jnp.inf, F32)
    for c in range(0, own, kc):
        s = dot(rows_of(kv_ref, 0, c, kc), q, NT)
        s_s[c : c + kc] = s
        top = jnp.maximum(top, jnp.max(s, axis=0, keepdims=True))
    norm = jnp.zeros((1, own), F32)
    mix = jnp.zeros((1, own), F32)
    for c in range(0, own, kc):
        e = jnp.exp2((s_s[c : c + kc] - top) * TO_EXP2)
        norm = norm + column_sum(e)
        mix = mix + column_sum(e * dot(rows_of(kv_ref, 1, c, kc), d, NT))
    stat_ref[0, 0:1] = top
    stat_ref[0, 1:2] = norm
    stat_ref[0, 2:3] = mix


def own_stats(kv, qd, kc=1024):
    _, pieces, nh, tok, _ = kv.shape
    own, width = pieces * tok, nh * HD
    return pl.pallas_call(
        functools.partial(own_stats_kernel, kc),
        grid=(nh,),
        out_shape=jax.ShapeDtypeStruct((nh, 8, own), F32),
        in_specs=[per_head(kv.shape), per_head(qd.shape)],
        out_specs=stat_block(own),
        scratch_shapes=[pltpu.VMEM((own, own), F32)],
        compiler_params=params(),
        cost_estimate=pl.CostEstimate(
            flops=4 * own * own * width, bytes_accessed=8 * own * width, transcendentals=own * own * nh
        ),
        name="own_stats",
    )(kv, qd)


def memory_kernel(tq, lists_ref, stat_ref, recv_ref, q_ref, d_ref, ret_ref, fin_ref, k_s, v_s, g_s):
    mem, own = k_s.shape[0], stat_ref.shape[2]
    memd = mem // FBLK
    count = lists_ref[memd]
    sure = LEAST_LIVE * FBLK
    load_memory(lists_ref, recv_ref, k_s, v_s)

    def products(t):
        q, d = rows_of(q_ref, 0, t, tq), rows_of(d_ref, 0, t, tq)
        s, dp = dot(k_s[...], q, NT), dot(v_s[...], d, NT)
        return q, d, jnp.concatenate([s[:sure], masked(s[sure:], count, sure)]), dp

    def terms(t, q, d, s, dp):
        qs = slice(t, t + tq)
        top_own = stat_ref[0, 0:1, qs]
        top = jnp.maximum(top_own, jnp.max(s, axis=0, keepdims=True))
        shrink = jnp.exp2((top_own - top) * TO_EXP2)
        e = jnp.exp2((s - top) * TO_EXP2)
        inv = 1.0 / (stat_ref[0, 1:2, qs] * shrink + column_sum(e))
        delta = (stat_ref[0, 2:3, qs] * shrink + column_sum(e * dp)) * inv
        fin_ref[0, 0:1, qs] = top
        fin_ref[0, 1:2, qs] = inv
        fin_ref[0, 2:3, qs] = delta
        p = e * inv
        gk = dot((p * (dp - delta)).astype(BF16), q, NN)
        gv = dot(p.astype(BF16), d, NN)
        g_s[0] = gk if t == 0 else g_s[0] + gk
        g_s[1] = gv if t == 0 else g_s[1] + gv

    ahead = products(0)
    for t in range(0, own, tq):
        now = ahead
        if t + tq < own:
            ahead = products(t + tq)
        terms(t, *now)
    for j in range(memd):
        rows = slice(j * FBLK, (j + 1) * FBLK)

        @pl.when(j < count)
        def _():
            ret_ref[lists_ref[j], 0] = (g_s[0, rows] * SCALE).astype(BF16)
            ret_ref[lists_ref[j], 1] = g_s[1, rows].astype(BF16)


def memory(lists, stat, recv, qd, tq=512):
    mem = (lists.shape[0] - 1) * FBLK
    nh, _, own = stat.shape
    width = nh * HD
    return pl.pallas_call(
        functools.partial(memory_kernel, tq),
        grid=(nh,),
        out_shape=(
            pltpu.HBM(recv.shape, BF16),
            jax.ShapeDtypeStruct((nh, 8, own), F32),
        ),
        in_specs=[smem(), stat_block(own), per_head(recv.shape), array_of(qd.shape, 0), array_of(qd.shape, 1)],
        out_specs=(per_head(recv.shape), stat_block(own)),
        scratch_shapes=[pltpu.VMEM((mem, HD), BF16)] * 2 + [pltpu.VMEM((2, mem, HD), F32)],
        compiler_params=params(MOST_VMEM),
        cost_estimate=pl.CostEstimate(
            flops=8 * own * mem * width, bytes_accessed=8 * own * width, transcendentals=own * mem * nh
        ),
        name="memory",
    )(lists, stat, recv, qd, qd)


def own_grads_kernel(kc, lists_ref, fin_ref, recv_ref, kv_ref, qd_ref, *refs):
    *dq_refs, own_ref, mk_s, mv_s = refs
    own, mem = fin_ref.shape[2], mk_s.shape[0]
    tok = own // len(dq_refs)
    load_memory(lists_ref, recv_ref, mk_s, mv_s)
    q, d = rows_of(qd_ref, 0, 0, own), rows_of(qd_ref, 1, 0, own)
    top, inv, delta = fin_ref[0, 0:1], fin_ref[0, 1:2], fin_ref[0, 2:3]

    def probabilities(k, v, count=None):
        s = dot(k, q, NT)
        if count is not None:
            s = masked(s, count)
        p = jnp.exp2((s - top) * TO_EXP2) * inv
        return p, (p * (dot(v, d, NT) - delta)).astype(BF16)

    _, ds = probabilities(mk_s[...], mv_s[...], lists_ref[mem // FBLK])
    dq = dot(ds, mk_s[...], TN)
    for c in range(0, own, kc):
        k, v = rows_of(kv_ref, 0, c, kc), rows_of(kv_ref, 1, c, kc)
        p, ds = probabilities(k, v)
        dq = dq + dot(ds, k, TN)
        own_ref[0, c : c + kc] = (dot(ds, q, NN) * SCALE).astype(BF16)
        own_ref[1, c : c + kc] = dot(p.astype(BF16), d, NN).astype(BF16)
    dq = (dq * SCALE).astype(BF16)
    for i, ref in enumerate(dq_refs):
        ref[0] = dq[i * tok : (i + 1) * tok]


def own_grads(lists, fin, recv, kv, qd, kc=1024):
    _, pieces, nh, tok, _ = kv.shape
    own, width = pieces * tok, nh * HD
    mem = (lists.shape[0] - 1) * FBLK
    total = own + mem
    piece, whole = (1, nh, tok, HD), (2, nh, own, HD)
    *dq, grads = pl.pallas_call(
        functools.partial(own_grads_kernel, kc),
        grid=(nh,),
        out_shape=[pltpu.HBM(piece, BF16)] * pieces + [pltpu.HBM(whole, BF16)],
        in_specs=[smem(), stat_block(own), per_head(recv.shape), per_head(kv.shape), per_head(qd.shape)],
        out_specs=[per_head(piece)] * pieces + [per_head(whole)],
        scratch_shapes=[pltpu.VMEM((mem, HD), BF16)] * 2,
        compiler_params=params(),
        cost_estimate=pl.CostEstimate(
            flops=10 * own * total * width, bytes_accessed=16 * own * width, transcendentals=own * total * nh
        ),
        name="own_grads",
    )(lists, fin, recv, kv, qd)
    return dq, grads


def collect_kernel(blocks_ref, own_ref, back_ref, *refs):
    *out_refs, acc = refs
    slots = back_ref.shape[0]
    tok = acc.shape[2] // len(out_refs)
    acc[...] = own_ref[...].astype(F32)
    for s in range(slots):

        @pl.when(blocks_ref[slots + s] != 0)
        def _():
            rows = pl.ds(pl.multiple_of(blocks_ref[s] * FBLK, FBLK), FBLK)
            acc[:, :, rows, :] += back_ref[s].astype(F32)

    for i, ref in enumerate(out_refs):
        ref[...] = acc[:, :, i * tok : (i + 1) * tok, :].astype(BF16)


def collect(blocks, own, back, pieces):
    _, nh, rows, _ = own.shape
    piece = (2, nh, rows // pieces, HD)
    return pl.pallas_call(
        collect_kernel,
        out_shape=[jax.ShapeDtypeStruct(piece, BF16)] * pieces,
        in_specs=[smem(), vmem(), vmem()],
        out_specs=[vmem()] * pieces,
        scratch_shapes=[pltpu.VMEM(own.shape, F32)],
        compiler_params=pltpu.CompilerParams(vmem_limit_bytes=SMALL_LIMIT),
        name="collect",
    )(blocks, own, back)


def pick_kernel(blocks_ref, kv_ref, out_ref, sems):
    per = kv_ref.shape[3] // FBLK
    copies = []
    for s in range(out_ref.shape[0]):
        block = blocks_ref[s]
        rows = pl.ds(pl.multiple_of(lax.rem(block, per) * FBLK, FBLK), FBLK)
        copies.append(
            pltpu.make_async_copy(kv_ref.at[:, lax.div(block, per), :, rows, :], out_ref.at[s], sems.at[s])
        )
    for copy in copies:
        copy.start()
    for copy in copies:
        copy.wait()


def pick(blocks, kv, slots):
    _, _, nh, _, _ = kv.shape
    return pl.pallas_call(
        pick_kernel,
        out_shape=pltpu.HBM((slots, 2, nh, FBLK, HD), BF16),
        in_specs=[smem(), vmem()],
        out_specs=anywhere(),
        scratch_shapes=[pltpu.SemaphoreType.DMA((slots,))],
        compiler_params=pltpu.CompilerParams(vmem_limit_bytes=SMALL_LIMIT),
        name="pick",
    )(blocks, kv)


def cut_kernel(me_ref, a_ref, b_ref, *refs):
    *out_refs, sems = refs
    count = len(out_refs)
    copies = []
    for k in (*ORDER, 0):
        heads = out_refs[k].shape[1]
        to = lax.rem(me_ref[0] + k, count)
        for h in range(heads):
            columns = pl.ds(pl.multiple_of((to * heads + h) * HD, HD), HD)
            for i, ref in enumerate((a_ref, b_ref)):
                copies.append(pltpu.make_async_copy(ref.at[:, columns], out_refs[k].at[i, h], sems.at[i, k, h]))
    for copy in copies:
        copy.start()
    for copy in copies:
        copy.wait()


def cut(me, a, b, count):
    tok, width = a.shape
    nh = width // count // HD
    return pl.pallas_call(
        cut_kernel,
        out_shape=[jax.ShapeDtypeStruct((2, nh, tok, HD), BF16)] * count,
        in_specs=[smem(), anywhere(), anywhere()],
        out_specs=[vmem()] * count,
        scratch_shapes=[pltpu.SemaphoreType.DMA((2, count, nh))],
        compiler_params=pltpu.CompilerParams(vmem_limit_bytes=MOST_VMEM),
        name="cut",
    )(me, a, b)


def place_kernel(ks, count, arrays, me_ref, *refs):
    out_refs, sems = refs[-1 - arrays : -1], refs[-1]
    copies = []
    for n, (k, ref) in enumerate(zip(ks, refs)):
        heads = ref.shape[1]
        of = lax.rem(me_ref[0] + k, count)
        for h in range(heads):
            columns = pl.ds(pl.multiple_of((of * heads + h) * HD, HD), HD)
            for i, out_ref in enumerate(out_refs):
                copies.append(pltpu.make_async_copy(ref.at[i, h], out_ref.at[:, columns], sems.at[i, n, h]))
    for copy in copies:
        copy.start()
    for copy in copies:
        copy.wait()


def place_some(me, pieces, ks, before):
    arrays, nh, tok, _ = pieces[0].shape
    count = len(pieces)
    return pl.pallas_call(
        functools.partial(place_kernel, ks, count, arrays),
        out_shape=[pltpu.HBM((tok, nh * HD * count), BF16)] * arrays,
        in_specs=[smem()] + [vmem()] * len(ks) + [anywhere()] * len(before),
        out_specs=[anywhere()] * arrays,
        input_output_aliases={1 + len(ks) + i: i for i in range(len(before))},
        scratch_shapes=[pltpu.SemaphoreType.DMA((arrays, len(ks), nh))],
        compiler_params=pltpu.CompilerParams(vmem_limit_bytes=SMALL_LIMIT),
        name="place",
    )(me, *(pieces[k] for k in ks), *before)


def place(me, pieces):
    early = (0, *ORDER[:-2])
    return place_some(me, pieces, ORDER[-2:], place_some(me, pieces, early, ()))


def shift(parts, sign):
    n = len(parts)
    got = {0: parts[0]}
    for k in ORDER:
        got[k] = lax.ppermute(parts[k], "head", [(i, (i + sign * k) % n) for i in range(n)])
    return [got[k] for k in range(n)]


def body(query, key, value, out_grad, intersection, counts):
    frames, heads = lax.axis_size("tok"), lax.axis_size("head")
    frame, me = lax.axis_index("tok"), lax.axis_index("head")
    me1 = me[None]
    blk_tok = query.shape[0] // FBLK
    blk_dev = blk_tok * heads
    slots = jnp.arange(intersection.shape[1], dtype=jnp.int32)
    live = slots[None, :] < counts[:, None]
    safe = jnp.maximum(intersection, 0)
    mine = live & (safe // blk_dev == frame)
    wanted = jnp.any(mine, axis=1).astype(jnp.int32)
    block = jnp.sum(jnp.where(mine, safe % blk_dev, 0), axis=1)
    piece = (me - block // blk_tok + heads) % heads
    blocks = jnp.concatenate([piece * blk_tok + block % blk_tok, wanted])
    my_ids = lax.dynamic_index_in_dim(safe, frame, 0, keepdims=False) // blk_dev
    my_count = lax.dynamic_index_in_dim(counts, frame, 0, keepdims=True)
    lists = jnp.concatenate([my_ids, my_count])

    kv = jnp.stack(shift(cut(me1, key, value, heads), 1), axis=1)
    sent = pick(blocks, kv, frames)
    query, out_grad, sent = lax.optimization_barrier((query, out_grad, sent))
    recv = lax.all_to_all(sent, "tok", split_axis=0, concat_axis=0, tiled=True)
    qd = jnp.stack(shift(cut(me1, query, out_grad, heads), 1), axis=1)
    stat = own_stats(kv, qd)
    ret, fin = memory(lists, stat, recv, qd)
    back = lax.all_to_all(ret, "tok", split_axis=0, concat_axis=0, tiled=True)
    dq, own = own_grads(lists, fin, recv, kv, qd)
    (dq_out,) = place(me1, shift(dq, -1))
    back, dq_out = lax.optimization_barrier((back, dq_out))
    dk_out, dv_out = place(me1, shift(collect(blocks, own, back, heads), -1))
    return (dq_out, dk_out, dv_out)


def solution(mesh):
    rows = P(("tok", "head"), None)
    return jax.shard_map(
        body,
        mesh=mesh,
        in_specs=(rows, rows, rows, rows, P(), P()),
        out_specs=(rows, rows, rows),
        check_vma=False,
    )
```
